256 devices in a mesh: tblk: 2 (over y_hi), chan: 128 (over y_lo, z, x, core).
Axes of the slice: x: 4, y: 4 (y_hi: 2, y_lo: 2; y = y_hi * 2 + y_lo), z: 8, core: 2. Of those that a mesh axis runs over, the one named last changes fastest.
Arguments:
- voltages: bfloat16 [8, 2, 1024, 32768], P(None, 'tblk', 'chan'), may hold values from -9 to 9
- input_gains: float32 [1024], P('chan'), may hold values from 0.5 to 2
Outputs:
- visibilities: bfloat16 [512, 2, 1024, 1024], P(('tblk', 'chan'))
The draws below stay inside these ranges and needn't reach their ends.
All inputs are finite; a program needn't handle non-finite values.
Results may differ from the reference program's by a relative error of at most 0.0054.
Values may be sent and summed in bfloat16 or wider, within the bound.
No kernel may reach another device: no remote copies, remote signals or barrier semaphores. Data moves between devices by JAX's collectives and lax.ppermute only.
A program may use at most 128 MiB of HBM per device.

```python
import math
import jax
import jax.numpy as jnp
from jax import lax

INPUTS = 1024
CHANNELS = 512
NFFT = 2048
TAPS = 4
SPEC = 16
BLK_DEV = 8
BLOCKS = 16
SPECTRA = 256
N_TBLK = 2


def draw_voltages(key, part):
    key = jax.random.fold_in(key, 11)
    noise_key, sky_key, couple_key = jax.random.split(key, 3)
    shape = (BLK_DEV, N_TBLK, INPUTS, SPEC * NFFT)
    noise = jnp.clip(jax.random.normal(noise_key, shape, jnp.float32), -4.0, 4.0)
    coupling = jax.random.uniform(couple_key, (INPUTS, 2), jnp.float32, -0.5, 0.5)
    sky = jnp.clip(jax.random.normal(sky_key, (BLK_DEV, N_TBLK, 2, SPEC * NFFT), jnp.float32), -4.0, 4.0)
    signal = noise + coupling[None, None, :, 0, None] * sky[:, :, 0:1, :] + coupling[None, None, :, 1, None] * sky[:, :, 1:2, :]
    return jnp.clip(signal, -9.0, 9.0).astype(jnp.bfloat16)


def block_scale(stream_key, shape, shards, low, high):
    def one(dim, parts):
        steps = jax.random.uniform(jax.random.fold_in(jax.random.fold_in(stream_key, 6), dim), (parts,), jnp.float32, low / len(shards), high / len(shards))
        return jnp.repeat(jnp.exp(steps), shape[dim] // parts).reshape((-1,) + (1,) * (len(shape) - dim - 1))

    level = one(*shards[0])
    for cut in shards[1:]:
        level = level * one(*cut)
    return level


def setup_inputs(seed: int = 0) -> dict:
    streams_of = jax.random.split(jax.random.key(seed), 3)
    return {
        "voltages": draw_voltages(jax.random.fold_in(streams_of[2], 71), 0),
        "input_gains": jnp.clip(jnp.exp(math.log(2.0) - 1.3862944 * jax.random.uniform(streams_of[1], (INPUTS,), jnp.float32) ** block_scale(streams_of[1], (INPUTS,), ((0, 128),), -0.2, 0.2)), 0.5, 2.0),
    }


def prototype(tap_count, fft_len):
    positions = jnp.arange(tap_count * fft_len, dtype=jnp.float32) + 0.5
    window = 0.5 - 0.5 * jnp.cos(2.0 * math.pi * positions / (tap_count * fft_len))
    shape_fn = jnp.sinc(positions / fft_len - tap_count / 2.0) * window
    shape_fn = shape_fn / jnp.sqrt(tap_count * jnp.mean(shape_fn * shape_fn))
    return shape_fn.reshape(tap_count, fft_len)

def make_table(chan_count, fft_len):
    chan_ids = jnp.arange(chan_count, dtype=jnp.int32)
    sample_ids = jnp.arange(fft_len, dtype=jnp.int32)
    phase = chan_ids[:, None] * sample_ids[None, :] % fft_len
    phase_angle = phase.astype(jnp.float32) * (2.0 * math.pi / fft_len)
    norm_scale = 1.0 / math.sqrt(fft_len)
    stacked = jnp.stack([jnp.cos(phase_angle) * norm_scale, -jnp.sin(phase_angle) * norm_scale], axis=1)
    return stacked.astype(jnp.bfloat16)

def reference(voltages, input_gains):
    frames = voltages.reshape(BLOCKS, INPUTS, SPEC, NFFT).transpose(1, 0, 2, 3).reshape(INPUTS, SPECTRA, NFFT)
    coefficients = prototype(TAPS, NFFT)
    dft_table = make_table(CHANNELS, NFFT).reshape(CHANNELS * 2, NFFT).T
    group_size = 64

    def transform(operands):
        group_frames, group_gains = operands
        extended = jnp.concatenate([jnp.zeros((group_size, TAPS - 1, NFFT), jnp.bfloat16), group_frames], axis=1)
        filtered_sum = jnp.zeros((group_size, SPECTRA, NFFT), jnp.float32)
        for tap_index in range(TAPS):
            filtered_sum = filtered_sum + coefficients[tap_index] * extended[:, tap_index:tap_index + SPECTRA].astype(jnp.float32)
        filtered = (filtered_sum * group_gains[:, None, None]).astype(jnp.bfloat16)
        spectra = jnp.dot(filtered.reshape(group_size * SPECTRA, NFFT), dft_table, preferred_element_type=jnp.float32)
        return spectra.astype(jnp.bfloat16).reshape(group_size, SPECTRA, CHANNELS, 2)
    spectra = lax.map(transform, (frames.reshape(INPUTS // group_size, group_size, SPECTRA, NFFT), input_gains.reshape(INPUTS // group_size, group_size)))
    spectra = spectra.reshape(INPUTS, SPECTRA, CHANNELS, 2)
    by_channel = spectra.transpose(2, 1, 3, 0)

    def correlate(channel_data):
        left_rows = channel_data.reshape(SPECTRA * 2, INPUTS)
        swapped = jnp.stack((channel_data[:, 1], -channel_data[:, 0]), axis=1).reshape(SPECTRA * 2, INPUTS)
        real_part = jnp.dot(left_rows.T, left_rows, preferred_element_type=jnp.float32)
        imag_part = jnp.dot(swapped.T, left_rows, preferred_element_type=jnp.float32)
        return (jnp.stack([real_part, imag_part]) * (1.0 / SPECTRA)).astype(jnp.bfloat16)
    return lax.map(correlate, by_channel)
```

```python
import functools
import math

import jax
import jax.numpy as jnp
import numpy as np
from jax import lax
from jax.experimental import pallas as pl
from jax.experimental.pallas import tpu as pltpu
from jax.sharding import PartitionSpec as P

CHANNELS = 512
NFFT = 2048
HALF = NFFT // 2
TAPS = 4
SPEC = 16
BLKS = 8
LANES = 128
SUB = 8
VMEM_LIMIT = 56 * 1024 * 1024


def prototype():
    positions = np.arange(TAPS * NFFT, dtype=np.float64) + 0.5
    window = 0.5 - 0.5 * np.cos(2.0 * math.pi * positions / (TAPS * NFFT))
    shape_fn = np.sinc(positions / NFFT - TAPS / 2.0) * window
    shape_fn = shape_fn / np.sqrt(TAPS * np.mean(shape_fn * shape_fn))
    return shape_fn.reshape(TAPS, NFFT).astype(np.float32)


def half_tables():
    chan = np.arange(CHANNELS, dtype=np.int64)
    sample = np.arange(HALF, dtype=np.int64)
    angle = (chan[:, None] * sample[None, :] % NFFT) * (2.0 * math.pi / NFFT)
    norm = 1.0 / math.sqrt(NFFT)
    real, imag = np.cos(angle) * norm, -np.sin(angle) * norm
    table = np.stack(
        [np.concatenate([real[r::2], imag[r::2]], axis=0) for r in range(2)]
    )
    return table.astype(jnp.bfloat16)


def filter_bank(place_ref, v_ref, gain_ref, coef_ref, table_ref, out_ref, frames, extra, rows, tiles):
    group = pl.program_id(0)
    first = 16 * group
    gain = gain_ref[...]
    slot = pl.multiple_of(first + SUB * place_ref[0], SUB)

    @pl.when(group == 0)
    def _():
        extra[...] = jnp.zeros_like(extra)

    def columns(j, carry):
        low = pl.multiple_of(j * LANES, LANES)
        weights = [
            [coef_ref[k : k + 1, pl.ds(low + h * HALF, LANES)] * gain for k in range(TAPS)]
            for h in range(2)
        ]
        window = [[None] * TAPS for _ in range(2)]
        for s in range(SPEC + TAPS - 1):
            sums = []
            for h in range(2):
                if s < SPEC:
                    now = v_ref[:, pl.ds(low + s * NFFT + h * HALF, LANES)].astype(jnp.float32)
                else:
                    now = None
                window[h] = window[h][1:] + [now]
                total = None
                for k in range(TAPS):
                    if window[h][k] is not None:
                        term = window[h][k] * weights[h][k]
                        total = term if total is None else total + term
                sums.append(total)
            pair = (sums[0] + sums[1], sums[0] - sums[1])
            for half in range(2):
                if s < SPEC:
                    frames[half, j, pl.ds(pl.multiple_of(s * 64 + first, 16), 16), :] = pair[half]
                else:
                    extra[half, j, pl.ds(pl.multiple_of((s - SPEC) * 80 + slot, SUB), 16), :] = pair[half]
        return carry

    lax.fori_loop(0, HALF // LANES, columns, 0)

    @pl.when(group == pl.num_programs(0) - 1)
    def _():
        lane = lax.broadcasted_iota(jnp.int32, (1, LANES), 1)
        dest = out_ref.shape[0]
        for part in range(2):
            base = 512 - 512 * part
            for half in range(2):
                for i in range(SUB):
                    for j in range(HALF // LANES):
                        picked = frames[half, j, pl.ds(base + i, 64, stride=SUB), :]
                        rows[i * 64 : (i + 1) * 64, j * LANES : (j + 1) * LANES] = picked.astype(jnp.bfloat16)
                spectra = lax.dot_general(
                    table_ref[half], rows[...], (((1,), (1,)), ((), ())),
                    preferred_element_type=jnp.float32,
                )
                for pair in range(SUB // 2):
                    real = spectra[:dest, pair * LANES : (pair + 1) * LANES]
                    imag = spectra[dest:, pair * LANES : (pair + 1) * LANES]
                    tiles[pl.ds(2 * pair, dest, stride=SUB), :] = jnp.where(
                        lane < 64, real, pltpu.roll(imag, 64, 1)
                    )
                    tiles[pl.ds(2 * pair + 1, dest, stride=SUB), :] = jnp.where(
                        lane < 64, pltpu.roll(real, 64, 1), imag
                    )
                out_ref[:, 2 * part + half] = tiles[...].reshape(dest, SUB, LANES).astype(jnp.bfloat16)
        parts = []
        for half in range(2):
            rows[...] = jnp.zeros_like(rows)
            for i in range(SUB):
                for j in range(HALF // LANES):
                    picked = jnp.concatenate(
                        [extra[half, j, pl.ds(80 * s + i, 8, stride=SUB), :] for s in range(TAPS - 1)]
                        + [jnp.zeros((8, LANES), jnp.float32)],
                        axis=0,
                    )
                    rows[i * 32 : (i + 1) * 32, j * LANES : (j + 1) * LANES] = picked.astype(jnp.bfloat16)
            spectra = lax.dot_general(
                table_ref[half], rows[:256], (((1,), (1,)), ((), ())),
                preferred_element_type=jnp.float32,
            )
            parts += [spectra[:dest], spectra[dest:]]
        for i in range(SUB):
            merged = None
            for slot_index in range(4):
                piece = parts[slot_index][:, (i // 4) * LANES : (i // 4 + 1) * LANES]
                shift = (32 * slot_index - 32 * (i % 4)) % LANES
                if shift:
                    piece = pltpu.roll(piece, shift, 1)
                merged = piece if merged is None else jnp.where(lane < 32 * slot_index, merged, piece)
            tiles[pl.ds(i, dest, stride=SUB), :] = merged
        out_ref[:, 4] = tiles[...].reshape(dest, SUB, LANES).astype(jnp.bfloat16)


def correlate(scale, recv_ref, out_ref, left, swap):
    item = pl.program_id(0)
    block = pl.program_id(1)
    count = left.shape[0]
    half = recv_ref.shape[0] // 2

    @pl.when(block == 0)
    def _():
        lane = lax.broadcasted_iota(jnp.int32, (1, LANES), 1)

        def put(column, piece):
            left[:, column * LANES : (column + 1) * LANES] = piece.astype(jnp.bfloat16)
            turned = pltpu.roll(piece, 64, 1)
            swap[:, column * LANES : (column + 1) * LANES] = jnp.where(lane < 64, turned, -turned).astype(jnp.bfloat16)

        def take(t, tile):
            return recv_ref[t * half : (t + 1) * half, tile].astype(jnp.float32).reshape(count, LANES)

        for t in range(2):
            put(2 * t, take(t, item))
            first = take(t, 2 + item)
            other = take(1 - t, 4)
            other = jnp.where(item == 0, other, pltpu.roll(other, 64, 1))
            other = jnp.where(
                lane < 32, other, jnp.where((lane >= 64) & (lane < 96), pltpu.roll(other, 32, 1), 0.0)
            )
            put(2 * t + 1, first + other)

    rows = out_ref.shape[2]
    at = pl.ds(pl.multiple_of(block * rows, rows), rows)
    for kind, source in enumerate((left, swap)):
        product = lax.dot_general(
            source[at, :], left[...], (((1,), (1,)), ((), ())), preferred_element_type=jnp.float32
        )
        out_ref[0, kind] = (product * scale).astype(jnp.bfloat16)


def on_device(voltages, input_gains):
    per_dev = voltages.shape[2]
    samples = voltages.shape[3]
    groups = lax.axis_size("tblk") * lax.axis_size("chan")
    inputs = lax.axis_size("chan") * per_dev
    coefs = jnp.asarray(prototype())
    table = jnp.asarray(half_tables())
    place = lax.axis_index("tblk").astype(jnp.int32).reshape(1)
    gain_rows = jnp.broadcast_to(jnp.tile(input_gains, 2)[:, None], (16, LANES))
    sent = pl.pallas_call(
        filter_bank,
        grid=(BLKS // 2,),
        in_specs=[
            pl.BlockSpec(memory_space=pltpu.SMEM),
            pl.BlockSpec((16, samples), lambda g: (g, 0)),
            pl.BlockSpec((16, LANES), lambda g: (0, 0)),
            pl.BlockSpec((TAPS, NFFT), lambda g: (0, 0)),
            pl.BlockSpec((2, CHANNELS, HALF), lambda g: (0, 0, 0)),
        ],
        out_specs=pl.BlockSpec((groups, 5, SUB, LANES), lambda g: (0, 0, 0, 0)),
        out_shape=jax.ShapeDtypeStruct((groups, 5, SUB, LANES), jnp.bfloat16),
        scratch_shapes=[
            pltpu.VMEM((2, HALF // LANES, SPEC * 64, LANES), jnp.float32),
            pltpu.VMEM((2, HALF // LANES, (TAPS - 1) * 80, LANES), jnp.float32),
            pltpu.VMEM((512, HALF), jnp.bfloat16),
            pltpu.VMEM((groups * SUB, LANES), jnp.float32),
        ],
        compiler_params=pltpu.CompilerParams(vmem_limit_bytes=VMEM_LIMIT),
        name="filter_bank",
    )(place, voltages.reshape(BLKS * per_dev, samples), gain_rows, coefs, table)
    turned = lax.all_to_all(sent, ("tblk", "chan"), split_axis=0, concat_axis=0, tiled=True)
    scale = 1.0 / (BLKS * SPEC * lax.axis_size("tblk"))
    items = CHANNELS // groups
    block = 256
    return pl.pallas_call(
        functools.partial(correlate, scale),
        grid=(items, inputs // block),
        in_specs=[pl.BlockSpec((groups, 5, SUB, LANES), lambda m, r: (0, 0, 0, 0))],
        out_specs=pl.BlockSpec((1, 2, block, inputs), lambda m, r: (m, 0, r, 0)),
        out_shape=jax.ShapeDtypeStruct((items, 2, inputs, inputs), jnp.bfloat16),
        scratch_shapes=[
            pltpu.VMEM((inputs, 4 * LANES), jnp.bfloat16),
            pltpu.VMEM((inputs, 4 * LANES), jnp.bfloat16),
        ],
        compiler_params=pltpu.CompilerParams(vmem_limit_bytes=VMEM_LIMIT),
        name="correlate",
    )(turned)


def solution(mesh):
    in_specs = (P(None, "tblk", "chan", None), P("chan"))
    out_specs = P(("tblk", "chan"), None, None, None)
    return jax.shard_map(
        on_device, mesh=mesh, in_specs=in_specs, out_specs=out_specs, check_vma=False
    )
```

```python
import functools
import math

import jax
import jax.numpy as jnp
import numpy as np
from jax import lax
from jax.experimental import pallas as pl
from jax.experimental.pallas import tpu as pltpu
from jax.sharding import Mesh, PartitionSpec as P

CHANNELS = 512
NFFT = 2048
HALF = NFFT // 2
TAPS = 4
SPEC = 16
BLKS = 8
LANES = 128
SUB = 8
RING = 8
AXES = ("yh", "yl", "z", "x", "c")
DEVICES = 256
FLAT = 32
MIB = 1024 * 1024
BF16 = jnp.bfloat16
F32 = jnp.float32


def prototype():
    positions = np.arange(TAPS * NFFT, dtype=np.float64) + 0.5
    window = 0.5 - 0.5 * np.cos(2.0 * math.pi * positions / (TAPS * NFFT))
    shape_fn = np.sinc(positions / NFFT - TAPS / 2.0) * window
    shape_fn = shape_fn / np.sqrt(TAPS * np.mean(shape_fn * shape_fn))
    return shape_fn.reshape(TAPS, NFFT).astype(np.float32)


def quarter_tables():
    owner = np.arange(DEVICES, dtype=np.int64).reshape(4, RING, 8).swapaxes(0, 1).reshape(DEVICES)
    sample = np.arange(HALF, dtype=np.int64)
    norm = 1.0 / math.sqrt(NFFT)
    quarters = []
    for r in range(2):
        angle = ((2 * owner[:, None] + r) * sample % NFFT) * (2.0 * math.pi / NFFT)
        quarters += [np.cos(angle) * norm, -np.sin(angle) * norm]
    return np.stack(quarters).astype(BF16)


def row_gain(gain_ref):
    row = lax.broadcasted_iota(jnp.int32, (2 * SUB, LANES), 0) % SUB
    gain = jnp.zeros((2 * SUB, LANES), F32)
    for i in range(SUB):
        gain = jnp.where(row == i, gain_ref[i], gain)
    return gain


def filter_frames(load, gain_ref, coef_ref, outputs, emit):
    gain = row_gain(gain_ref)

    def columns(j, carry):
        low = pl.multiple_of(j * LANES, LANES)
        weights = [
            [coef_ref[k : k + 1, pl.ds(low + h * HALF, LANES)] * gain for k in range(TAPS)]
            for h in range(2)
        ]
        held = {}
        for s in outputs:
            sums = []
            for h in range(2):
                total = None
                for k in range(TAPS):
                    frame = s - (TAPS - 1) + k
                    if frame < 0 or frame >= SPEC:
                        continue
                    if (frame, h) not in held:
                        held[frame, h] = load(frame, low + h * HALF).astype(F32)
                    term = held[frame, h] * weights[h][k]
                    total = term if total is None else total + term
                sums.append(total)
            emit(s, j, sums[0] + sums[1], sums[0] - sums[1])
        return carry

    lax.fori_loop(0, HALF // LANES, columns, 0)


def place_rows(rows, half, group, i, j, picked):
    packed = picked.astype(BF16)
    for q in (2 * half, 2 * half + 1):
        at = group * 256 + (i // 4) * LANES + ((i + q) % 4) * 32
        rows[q, at : at + 32, j * LANES : (j + 1) * LANES] = packed


def transform(table, half, rows, spec):
    for q in (2 * half, 2 * half + 1):
        spec[q] = lax.dot_general(
            table[q], rows[q], (((1,), (1,)), ((), ())), preferred_element_type=F32
        )


def owner_tiles(spec, tiles, group, turn, start, count):
    lane = lax.broadcasted_iota(jnp.int32, (1, LANES), 1)
    for i in range(SUB):
        p = i % 4
        at = group * 256 + (i // 4) * LANES
        merged = None
        for r in range(4):
            piece = spec[(r - p) % 4, pl.ds(start, count), at : at + LANES]
            merged = piece if merged is None else jnp.where(lane < 32 * r, merged, piece)
        if (turn - p) % 4:
            merged = pltpu.roll(merged, 32 * ((turn - p) % 4), 1)
        tiles[pl.ds(i, count, stride=SUB), :] = merged


def last_frames(y_ref, z_ref, c_ref, gain_ref, high_ref, mid_ref, coef_ref, table_ref,
                own_ref, other_ref, far_ref, near_ref, tail_ref, frames, extra, rows, spec, tiles, held, sem):
    step = pl.program_id(0)
    slot_row = pl.multiple_of(16 * step + SUB * (y_ref[0] >> 1), SUB)
    fetch = pltpu.make_async_copy(table_ref, held, sem)

    @pl.when(step == 0)
    def _():
        fetch.start()
        extra[...] = jnp.zeros_like(extra)

    def load(frame, low):
        if frame >= 12:
            return high_ref[:, pl.ds(low + (frame - 12) * NFFT, LANES)]
        return mid_ref[:, pl.ds(low + (frame - 8) * NFFT, LANES)]

    def emit(s, j, total, diff):
        if s < SPEC:
            at = pl.ds(pl.multiple_of((s - 12) * 64 + 16 * step, 16), 16)
            frames[0, j, at, :] = total
            frames[1, j, at, :] = diff
        else:
            at = pl.ds(pl.multiple_of((s - SPEC) * 80 + slot_row, SUB), 16)
            extra[0, j, at, :] = total
            extra[1, j, at, :] = diff

    filter_frames(load, gain_ref, coef_ref, range(12, SPEC + TAPS - 1), emit)

    @pl.when(step == pl.num_programs(0) - 1)
    def _():
        for half in range(2):
            for i in range(SUB):
                for j in range(HALF // LANES):
                    place_rows(rows, half, 0, i, j, frames[half, j, pl.ds(i, 32, stride=SUB), :])
                    picked = jnp.concatenate(
                        [extra[half, j, pl.ds(80 * s + i, 8, stride=SUB), :] for s in range(TAPS - 1)]
                        + [jnp.zeros((8, LANES), F32)],
                        axis=0,
                    )
                    place_rows(rows, half, 1, i, j, picked)
            if half == 0:
                fetch.wait()
            transform(held, half, rows, spec)
        core = c_ref[0]
        sign = 1 - 2 * core
        for slot, away in enumerate((1, 2, 3, -1, -2, -3, 4, 0)):
            zdest = (z_ref[0] + (sign * away if slot < 6 else away) + RING) & (RING - 1)
            tile = tiles.at[slot]
            owner_tiles(spec, tile, 0, 3, pl.multiple_of(zdest * FLAT, FLAT), FLAT)
            parts = tile[...].reshape(FLAT // 2, 2, SUB, LANES).astype(BF16)
            if slot < 3:
                for owner_core in range(2):
                    own_ref[slot, owner_core] = parts[:, owner_core]
            elif slot < 6:
                for owner_core in range(2):
                    other_ref[slot - 3, owner_core] = parts[:, owner_core]
            else:
                kept_ref = far_ref if slot == 6 else near_ref
                for owner_core in range(2):
                    @pl.when(core == owner_core)
                    def _(owner_core=owner_core):
                        kept_ref[...] = parts[:, owner_core]
                        other_ref[3, slot - 6] = parts[:, 1 - owner_core]
        store_owners(spec, tiles, 8, 1, 0, tail_ref)


def store_owners(spec, tiles, first, group, turn, out_ref):
    for z in range(RING):
        tile = tiles.at[first + z]
        owner_tiles(spec, tile, group, turn, z * FLAT, FLAT)
        out_ref[:, z] = tile[...].reshape(4, SUB, SUB, LANES).astype(BF16)


def main_frames(gain_ref, low_ref, mid_ref, coef_ref, table_ref, out_ref, frames, rows, spec, tiles, held, sem):
    step = pl.program_id(0)
    fetch = pltpu.make_async_copy(table_ref, held, sem)
    pl.when(step == 0)(fetch.start)

    def load(frame, low):
        if frame < 8:
            return low_ref[:, pl.ds(low + frame * NFFT, LANES)]
        return mid_ref[:, pl.ds(low + (frame - 8) * NFFT, LANES)]

    def emit(s, j, total, diff):
        at = pl.ds(pl.multiple_of(s * 64 + 16 * step, 16), 16)
        frames[0, j, at, :] = total
        frames[1, j, at, :] = diff

    filter_frames(load, gain_ref, coef_ref, range(12), emit)

    @pl.when(step == pl.num_programs(0) - 1)
    def _():
        for half in range(2):
            for group in range(3):
                for i in range(SUB):
                    for j in range(HALF // LANES):
                        picked = frames[half, j, pl.ds(group * 256 + i, 32, stride=SUB), :]
                        place_rows(rows, half, group, i, j, picked)
            if half == 0:
                fetch.wait()
            transform(held, half, rows, spec)
        for group in range(3):
            store_owners(spec, tiles, RING * group, group, group, out_ref.at[group])


def complete(main_ref, tail_ref, out_ref):
    first = main_ref[0].astype(F32) + tail_ref[...].astype(F32)
    out_ref[:, 0] = first.astype(BF16)
    for group in range(1, 3):
        out_ref[:, group] = main_ref[group]


def sort_y(y_ref, c_ref, one_ref, two_ref, three_ref, part_ref, far_ref, near_ref, next_ref,
           out0_ref, out1_ref, out2_ref, out3_ref):
    core = c_ref[0]
    for dy, out_ref in enumerate((out0_ref, out1_ref, out2_ref, out3_ref)):
        at = pl.ds(((y_ref[0] + dy) & 3) * 4, 4)
        for j, ref in enumerate((one_ref, two_ref, three_ref)):
            for r in range(2):
                out_ref[2 * j + r] = ref[core, r, at]
                out_ref[6 + 2 * j + r] = part_ref[j, r, at]
        for r in range(2):
            out_ref[12 + r] = far_ref[r, at]
        out_ref[14] = near_ref[at]
        out_ref[15] = next_ref[at]


def sort_x(x_ref, a0_ref, a1_ref, a2_ref, a3_ref, out0_ref, out1_ref, out2_ref, out3_ref):
    for dx, out_ref in enumerate((out0_ref, out1_ref, out2_ref, out3_ref)):
        owner_x = (x_ref[0] + dx) & 3
        for dy, ref in enumerate((a0_ref, a1_ref, a2_ref, a3_ref)):
            out_ref[dy] = ref[:, owner_x]


def arrange(y_ref, z_ref, x_ref, c_ref, a0_ref, a1_ref, a2_ref, a3_ref, out_ref):
    y, z, x, core = y_ref[0], z_ref[0], x_ref[0], c_ref[0]
    sign = 1 - 2 * core
    origin = []
    for j in range(3):
        origin += [(-sign * (j + 1), core), (-sign * (j + 1), 1 - core)]
    for j in range(3):
        origin += [(sign * (j + 1), 1 - core), (sign * (j + 1), core)]
    origin += [(4, core), (4, 1 - core), (0, core), (0, 1 - core)]
    for dx, ref in enumerate((a0_ref, a1_ref, a2_ref, a3_ref)):
        xsrc = (x - dx + 4) & 3
        for dy in range(4):
            ysrc = (y - dy + 4) & 3
            for k, (away, source_core) in enumerate(origin):
                zsrc = (z + away + RING) & (RING - 1)
                out_ref[((ysrc * RING + zsrc) * 4 + xsrc) * 2 + source_core] = ref[dy, k]


def correlate(scale, main_ref, last_ref, out_ref, left, swap):
    item = pl.program_id(0)
    block = pl.program_id(1)
    half = DEVICES // 2

    def collect(which):
        lane = lax.broadcasted_iota(jnp.int32, (1, LANES), 1)
        rows = left.shape[0]
        for t in range(2):
            here = slice(t * half, (t + 1) * half)
            groups = [main_ref[here, g] for g in range(3)] + [last_ref[here]]
            groups = [g.astype(F32).reshape(rows, LANES) for g in groups]

            def quarter(q):
                merged = None
                for r in range(4):
                    piece = groups[(r - q) % 4]
                    merged = piece if merged is None else jnp.where(lane < 32 * r, merged, piece)
                return merged

            real = quarter(2 * which)
            imag = pltpu.roll(quarter(2 * which + 1), LANES - 32, 1)
            first = slice(2 * t * LANES, (2 * t + 1) * LANES)
            second = slice((2 * t + 1) * LANES, (2 * t + 2) * LANES)
            left[:, first] = real.astype(BF16)
            swap[:, second] = (-real).astype(BF16)
            imag = imag.astype(BF16)
            left[:, second] = imag
            swap[:, first] = imag

    for which in range(2):
        pl.when((block == 0) & (item == which))(functools.partial(collect, which))

    count = out_ref.shape[2]
    at = pl.ds(pl.multiple_of(block * count, count), count)
    for kind, source in enumerate((left, swap)):
        product = lax.dot_general(
            source[at, :], left[...], (((1,), (1,)), ((), ())), preferred_element_type=F32
        )
        out_ref[0, kind] = (product * scale).astype(BF16)


def along_ring(block, distance):
    route = []
    for z in range(RING):
        for c in range(2):
            target = (z + (distance if c == 0 else -distance)) % RING
            route.append((z * 2 + c, target * 2 + c))
    return lax.ppermute(block, ("z", "c"), route)


def along(block, axis, distance, size):
    return lax.ppermute(block, axis, [(i, (i + distance) % size) for i in range(size)])


def call(kernel, grid, in_specs, out_specs, out_shape, scratch, name, limit):
    return pl.pallas_call(
        kernel, grid=grid, in_specs=in_specs, out_specs=out_specs, out_shape=out_shape,
        scratch_shapes=scratch, name=name,
        compiler_params=pltpu.CompilerParams(vmem_limit_bytes=limit * MIB),
    )


def whole(*shape):
    return pl.BlockSpec(shape, lambda *ids: (0,) * len(shape))


SMEM = pl.BlockSpec(memory_space=pltpu.SMEM)


def simple(kernel, scalars, arrays, shapes, name):
    return call(
        kernel, (1,), [SMEM] * len(scalars) + [whole(*a.shape) for a in arrays],
        [whole(*s) for s in shapes], [jax.ShapeDtypeStruct(s, BF16) for s in shapes], [], name, 8,
    )(*scalars, *arrays)


def on_device(voltages, input_gains):
    per_dev = voltages.shape[2]
    samples = voltages.shape[3]
    inputs = 128 * per_dev
    coefs = jnp.asarray(prototype())
    table = jnp.asarray(quarter_tables())
    y, z, x, core = [
        lax.axis_index(a).astype(jnp.int32).reshape(1) for a in (("yh", "yl"), "z", "x", "c")
    ]
    stream = voltages.reshape(BLKS * per_dev, samples)
    quarter = samples // 4
    tile = (SUB, LANES)
    tables = [whole(TAPS, NFFT), pl.BlockSpec(memory_space=pl.ANY)]
    table_scratch = [pltpu.VMEM((4, DEVICES, HALF), BF16), pltpu.SemaphoreType.DMA]

    slab = (FLAT // 2,) + tile
    owners = (4, RING, SUB) + tile
    last_shapes = [(3, 2) + slab, (4, 2) + slab, slab, slab, owners]
    own, other, far, near, tail = call(
        last_frames, (BLKS // 2,),
        [
            SMEM, SMEM, SMEM, SMEM,
            pl.BlockSpec((16, quarter), lambda g: (g, 3)),
            pl.BlockSpec((16, quarter), lambda g: (g, 2)),
        ] + tables,
        [whole(*s) for s in last_shapes], [jax.ShapeDtypeStruct(s, BF16) for s in last_shapes],
        [
            pltpu.VMEM((2, HALF // LANES, 256, LANES), F32),
            pltpu.VMEM((2, HALF // LANES, (TAPS - 1) * 80, LANES), F32),
            pltpu.VMEM((4, 512, HALF), BF16),
            pltpu.VMEM((4, DEVICES, 512), F32),
            pltpu.VMEM((16, FLAT * SUB, LANES), F32),
        ] + table_scratch,
        "last_frames", 56,
    )(y, z, core, input_gains, stream, stream, coefs, table)
    tail = along(tail, "yh", 1, 2)
    other = along(other, "c", 1, 2)
    main_gains, other = lax.optimization_barrier((input_gains, other))
    far = along_ring(jnp.stack([far, other[3, 0]]), 4)
    ring = [along_ring(jnp.stack([own[j], other[j]], axis=1), j + 1) for j in range(3)]

    main = call(
        main_frames, (BLKS // 2,),
        [
            SMEM,
            pl.BlockSpec((16, 2 * quarter), lambda g: (g, 0)),
            pl.BlockSpec((16, quarter), lambda g: (g, 2)),
        ] + tables,
        whole(3, *owners), jax.ShapeDtypeStruct((3,) + owners, BF16),
        [
            pltpu.VMEM((2, HALF // LANES, 768, LANES), F32),
            pltpu.VMEM((4, 768, HALF), BF16),
            pltpu.VMEM((4, DEVICES, 768), F32),
            pltpu.VMEM((3 * RING, FLAT * SUB, LANES), F32),
        ] + table_scratch,
        "main_frames", 56,
    )(main_gains, stream, stream, coefs, table)
    ring, far, tail, main = lax.optimization_barrier((ring, far, tail, main))
    packed = (DEVICES, 3) + tile
    main, = simple(
        complete, (), (main.reshape((3, DEVICES) + tile), tail.reshape((DEVICES,) + tile)), [packed], "complete"
    )
    main = lax.all_to_all(main, AXES, split_axis=0, concat_axis=0, tiled=True)

    leaving = jnp.stack([lax.dynamic_index_in_dim(a, 1 - core[0], 0, keepdims=False) for a in ring])
    part = along(leaving, "c", 1, 2)
    by_y = simple(
        sort_y, (y, core), (*ring, part, far, near, other[3, 1]), [(16, 4) + tile] * 4, "sort_y"
    )
    by_y = [by_y[0]] + [along(by_y[d], ("yh", "yl"), d, 4) for d in range(1, 4)]
    by_x = simple(sort_x, (x,), by_y, [(4, 16) + tile] * 4, "sort_x")
    by_x = [by_x[0]] + [along(by_x[d], "x", d, 4) for d in range(1, 4)]
    last, = simple(arrange, (y, z, x, core), by_x, [(DEVICES,) + tile], "arrange")

    scale = 1.0 / (BLKS * SPEC * lax.axis_size("yh"))
    block = 512
    return call(
        functools.partial(correlate, scale), (2, inputs // block),
        [whole(*packed), whole(DEVICES, *tile)],
        pl.BlockSpec((1, 2, block, inputs), lambda m, r: (m, 0, r, 0)),
        jax.ShapeDtypeStruct((2, 2, inputs, inputs), BF16),
        [pltpu.VMEM((inputs, 4 * LANES), BF16), pltpu.VMEM((inputs, 4 * LANES), BF16)],
        "correlate", 28,
    )(main, last)


def solution(mesh):
    fine = Mesh(mesh.devices.reshape(2, 2, RING, 4, 2), AXES)
    inputs = ("yl", "z", "x", "c")
    return jax.shard_map(
        on_device, mesh=fine, in_specs=(P(None, "yh", inputs, None), P(inputs)),
        out_specs=P(AXES, None, None, None), check_vma=False,
    )
```

```python
import functools
import math

import jax
import jax.numpy as jnp
import numpy as np
from jax import lax
from jax.experimental import pallas as pl
from jax.experimental.pallas import tpu as pltpu
from jax.sharding import Mesh, PartitionSpec as P

CHANNELS = 512
NFFT = 2048
HALF = NFFT // 2
TAPS = 4
SPEC = 16
BLKS = 8
LANES = 128
SUB = 8
RING = 8
AXES = ("yh", "yl", "z", "x", "c")
DEVICES = 256
FLAT = 32
MIB = 1024 * 1024
BF16 = jnp.bfloat16
F32 = jnp.float32


def prototype():
    positions = np.arange(TAPS * NFFT, dtype=np.float64) + 0.5
    window = 0.5 - 0.5 * np.cos(2.0 * math.pi * positions / (TAPS * NFFT))
    shape_fn = np.sinc(positions / NFFT - TAPS / 2.0) * window
    shape_fn = shape_fn / np.sqrt(TAPS * np.mean(shape_fn * shape_fn))
    return shape_fn.reshape(TAPS, NFFT).astype(np.float32)


def quarter_tables():
    owner = np.arange(DEVICES, dtype=np.int64).reshape(4, RING, 8).swapaxes(0, 1).reshape(DEVICES)
    sample = np.arange(HALF, dtype=np.int64)
    norm = 1.0 / math.sqrt(NFFT)
    quarters = []
    for r in range(2):
        angle = ((2 * owner[:, None] + r) * sample % NFFT) * (2.0 * math.pi / NFFT)
        quarters += [np.cos(angle) * norm, -np.sin(angle) * norm]
    return np.stack(quarters).astype(BF16)


def row_gain(gain_ref):
    row = lax.broadcasted_iota(jnp.int32, (2 * SUB, LANES), 0) % SUB
    gain = jnp.zeros((2 * SUB, LANES), F32)
    for i in range(SUB):
        gain = jnp.where(row == i, gain_ref[i], gain)
    return gain


def filter_frames(load, gain_ref, coef_ref, outputs, emit):
    gain = row_gain(gain_ref)

    def columns(j, carry):
        low = pl.multiple_of(j * LANES, LANES)
        weights = [
            [coef_ref[k : k + 1, pl.ds(low + h * HALF, LANES)] * gain for k in range(TAPS)]
            for h in range(2)
        ]
        held = {}
        for s in outputs:
            sums = []
            for h in range(2):
                total = None
                for k in range(TAPS):
                    frame = s - (TAPS - 1) + k
                    if frame < 0 or frame >= SPEC:
                        continue
                    if (frame, h) not in held:
                        held[frame, h] = load(frame, low + h * HALF).astype(F32)
                    term = held[frame, h] * weights[h][k]
                    total = term if total is None else total + term
                sums.append(total)
            emit(s, j, sums[0] + sums[1], sums[0] - sums[1])
        return carry

    lax.fori_loop(0, HALF // LANES, columns, 0)


def place_rows(rows, half, group, i, j, picked):
    packed = picked.astype(BF16)
    for q in (2 * half, 2 * half + 1):
        at = group * 256 + (i // 4) * LANES + ((i + q) % 4) * 32
        rows[q, at : at + 32, j * LANES : (j + 1) * LANES] = packed


def transform(table, half, rows, spec):
    for q in (2 * half, 2 * half + 1):
        spec[q] = lax.dot_general(
            table[q], rows[q], (((1,), (1,)), ((), ())), preferred_element_type=F32
        )


def owner_tiles(spec, tiles, group, turn, start, count):
    lane = lax.broadcasted_iota(jnp.int32, (1, LANES), 1)
    for i in range(SUB):
        p = i % 4
        at = group * 256 + (i // 4) * LANES
        merged = None
        for r in range(4):
            piece = spec[(r - p) % 4, pl.ds(start, count), at : at + LANES]
            merged = piece if merged is None else jnp.where(lane < 32 * r, merged, piece)
        if (turn - p) % 4:
            merged = pltpu.roll(merged, 32 * ((turn - p) % 4), 1)
        tiles[pl.ds(i, count, stride=SUB), :] = merged


def last_frames(y_ref, z_ref, c_ref, gain_ref, high_ref, mid_ref, coef_ref, table_ref,
                own_ref, other_ref, far_ref, near_ref, tail_ref, frames, extra, rows, spec, tiles, held, sem):
    step = pl.program_id(0)
    slot_row = pl.multiple_of(16 * step + SUB * (y_ref[0] >> 1), SUB)
    fetch = pltpu.make_async_copy(table_ref, held, sem)

    @pl.when(step == 0)
    def _():
        fetch.start()
        extra[...] = jnp.zeros_like(extra)

    def load(frame, low):
        if frame >= 12:
            return high_ref[:, pl.ds(low + (frame - 12) * NFFT, LANES)]
        return mid_ref[:, pl.ds(low + (frame - 8) * NFFT, LANES)]

    def emit(s, j, total, diff):
        if s < SPEC:
            at = pl.ds(pl.multiple_of((s - 12) * 64 + 16 * step, 16), 16)
            frames[0, j, at, :] = total
            frames[1, j, at, :] = diff
        else:
            at = pl.ds(pl.multiple_of((s - SPEC) * 80 + slot_row, SUB), 16)
            extra[0, j, at, :] = total
            extra[1, j, at, :] = diff

    filter_frames(load, gain_ref, coef_ref, range(12, SPEC + TAPS - 1), emit)

    @pl.when(step == pl.num_programs(0) - 1)
    def _():
        for half in range(2):
            for i in range(SUB):
                for j in range(HALF // LANES):
                    place_rows(rows, half, 0, i, j, frames[half, j, pl.ds(i, 32, stride=SUB), :])
                    picked = jnp.concatenate(
                        [extra[half, j, pl.ds(80 * s + i, 8, stride=SUB), :] for s in range(TAPS - 1)]
                        + [jnp.zeros((8, LANES), F32)],
                        axis=0,
                    )
                    place_rows(rows, half, 1, i, j, picked)
            if half == 0:
                fetch.wait()
            transform(held, half, rows, spec)
        core = c_ref[0]
        sign = 1 - 2 * core
        for slot, away in enumerate((1, 2, 3, -1, -2, -3, 4, 0)):
            zdest = (z_ref[0] + (sign * away if slot < 6 else away) + RING) & (RING - 1)
            tile = tiles.at[slot]
            owner_tiles(spec, tile, 0, 3, pl.multiple_of(zdest * FLAT, FLAT), FLAT)
            parts = tile[...].reshape(FLAT // 2, 2, SUB, LANES).astype(BF16)
            if slot < 3:
                for owner_core in range(2):
                    own_ref[slot, owner_core] = parts[:, owner_core]
            elif slot < 6:
                for owner_core in range(2):
                    other_ref[slot - 3, owner_core] = parts[:, owner_core]
            else:
                kept_ref = far_ref if slot == 6 else near_ref
                for owner_core in range(2):
                    @pl.when(core == owner_core)
                    def _(owner_core=owner_core):
                        kept_ref[...] = parts[:, owner_core]
                        other_ref[3, slot - 6] = parts[:, 1 - owner_core]
        store_owners(spec, tiles, 8, 1, 0, tail_ref)


def store_owners(spec, tiles, first, group, turn, out_ref):
    for z in range(RING):
        tile = tiles.at[first + z]
        owner_tiles(spec, tile, group, turn, z * FLAT, FLAT)
        out_ref[:, z] = tile[...].reshape(4, SUB, SUB, LANES).astype(BF16)


def main_frames(gain_ref, low_ref, mid_ref, coef_ref, table_ref, out_ref, frames, rows, spec, tiles, held, sem):
    step = pl.program_id(0)
    fetch = pltpu.make_async_copy(table_ref, held, sem)
    pl.when(step == 0)(fetch.start)

    def load(frame, low):
        if frame < 8:
            return low_ref[:, pl.ds(low + frame * NFFT, LANES)]
        return mid_ref[:, pl.ds(low + (frame - 8) * NFFT, LANES)]

    def emit(s, j, total, diff):
        at = pl.ds(pl.multiple_of(s * 64 + 16 * step, 16), 16)
        frames[0, j, at, :] = total
        frames[1, j, at, :] = diff

    filter_frames(load, gain_ref, coef_ref, range(12), emit)

    @pl.when(step == pl.num_programs(0) - 1)
    def _():
        for half in range(2):
            for group in range(3):
                for i in range(SUB):
                    for j in range(HALF // LANES):
                        picked = frames[half, j, pl.ds(group * 256 + i, 32, stride=SUB), :]
                        place_rows(rows, half, group, i, j, picked)
            if half == 0:
                fetch.wait()
            transform(held, half, rows, spec)
        for group in range(3):
            store_owners(spec, tiles, RING * group, group, group, out_ref.at[group])


def complete(main_ref, tail_ref, out_ref):
    first = main_ref[0].astype(F32) + tail_ref[...].astype(F32)
    out_ref[:, 0] = first.astype(BF16)
    for group in range(1, 3):
        out_ref[:, group] = main_ref[group]


def sort_y(y_ref, c_ref, one_ref, two_ref, three_ref, part_ref, far_ref, near_ref, next_ref,
           out0_ref, out1_ref, out2_ref, out3_ref):
    core = c_ref[0]
    for dy, out_ref in enumerate((out0_ref, out1_ref, out2_ref, out3_ref)):
        at = pl.ds(((y_ref[0] + dy) & 3) * 4, 4)
        for j, ref in enumerate((one_ref, two_ref, three_ref)):
            for r in range(2):
                out_ref[2 * j + r] = ref[core, r, at]
                out_ref[6 + 2 * j + r] = part_ref[j, r, at]
        for r in range(2):
            out_ref[12 + r] = far_ref[r, at]
        out_ref[14] = near_ref[at]
        out_ref[15] = next_ref[at]


def sort_x(x_ref, a0_ref, a1_ref, a2_ref, a3_ref, out0_ref, out1_ref, out2_ref, out3_ref):
    for dx, out_ref in enumerate((out0_ref, out1_ref, out2_ref, out3_ref)):
        owner_x = (x_ref[0] + dx) & 3
        for dy, ref in enumerate((a0_ref, a1_ref, a2_ref, a3_ref)):
            out_ref[dy] = ref[:, owner_x]


def arrange(y_ref, z_ref, x_ref, c_ref, a0_ref, a1_ref, a2_ref, a3_ref, out_ref):
    y, z, x, core = y_ref[0], z_ref[0], x_ref[0], c_ref[0]
    sign = 1 - 2 * core
    origin = []
    for j in range(3):
        origin += [(-sign * (j + 1), core), (-sign * (j + 1), 1 - core)]
    for j in range(3):
        origin += [(sign * (j + 1), 1 - core), (sign * (j + 1), core)]
    origin += [(4, core), (4, 1 - core), (0, core), (0, 1 - core)]
    for dx, ref in enumerate((a0_ref, a1_ref, a2_ref, a3_ref)):
        xsrc = (x - dx + 4) & 3
        for dy in range(4):
            ysrc = (y - dy + 4) & 3
            for k, (away, source_core) in enumerate(origin):
                zsrc = (z + away + RING) & (RING - 1)
                out_ref[((ysrc * RING + zsrc) * 4 + xsrc) * 2 + source_core] = ref[dy, k]


def correlate(scale, main_ref, last_ref, out_ref, left, swap):
    item = pl.program_id(0)
    block = pl.program_id(1)
    half = DEVICES // 2

    def collect(which):
        lane = lax.broadcasted_iota(jnp.int32, (1, LANES), 1)
        rows = left.shape[0]
        for t in range(2):
            here = slice(t * half, (t + 1) * half)
            groups = [main_ref[here, g] for g in range(3)] + [last_ref[here]]
            groups = [g.astype(F32).reshape(rows, LANES) for g in groups]

            def quarter(q):
                merged = None
                for r in range(4):
                    piece = groups[(r - q) % 4]
                    merged = piece if merged is None else jnp.where(lane < 32 * r, merged, piece)
                return merged

            real = quarter(2 * which)
            imag = pltpu.roll(quarter(2 * which + 1), LANES - 32, 1)
            first = slice(2 * t * LANES, (2 * t + 1) * LANES)
            second = slice((2 * t + 1) * LANES, (2 * t + 2) * LANES)
            left[:, first] = real.astype(BF16)
            swap[:, second] = (-real).astype(BF16)
            imag = imag.astype(BF16)
            left[:, second] = imag
            swap[:, first] = imag

    for which in range(2):
        pl.when((block == 0) & (item == which))(functools.partial(collect, which))

    count = out_ref.shape[2]
    at = pl.ds(pl.multiple_of(block * count, count), count)
    for kind, source in enumerate((left, swap)):
        product = lax.dot_general(
            source[at, :], left[...], (((1,), (1,)), ((), ())), preferred_element_type=F32
        )
        out_ref[0, kind] = (product * scale).astype(BF16)


def along_ring(block, distance):
    route = []
    for z in range(RING):
        for c in range(2):
            target = (z + (distance if c == 0 else -distance)) % RING
            route.append((z * 2 + c, target * 2 + c))
    return lax.ppermute(block, ("z", "c"), route)


def along(block, axis, distance, size):
    return lax.ppermute(block, axis, [(i, (i + distance) % size) for i in range(size)])


def call(kernel, grid, in_specs, out_specs, out_shape, scratch, name, limit):
    return pl.pallas_call(
        kernel, grid=grid, in_specs=in_specs, out_specs=out_specs, out_shape=out_shape,
        scratch_shapes=scratch, name=name,
        compiler_params=pltpu.CompilerParams(vmem_limit_bytes=limit * MIB),
    )


def whole(*shape):
    return pl.BlockSpec(shape, lambda *ids: (0,) * len(shape))


SMEM = pl.BlockSpec(memory_space=pltpu.SMEM)
IN_VMEM = pl.BlockSpec(memory_space=pltpu.VMEM)


def in_vmem(array):
    return pltpu.with_memory_space_constraint(array, pltpu.VMEM)


def simple(kernel, scalars, arrays, shapes, name):
    return call(
        kernel, (1,), [SMEM] * len(scalars) + [whole(*a.shape) for a in arrays],
        [whole(*s) for s in shapes], [jax.ShapeDtypeStruct(s, BF16) for s in shapes], [], name, 8,
    )(*scalars, *arrays)


def on_device(voltages, input_gains):
    per_dev = voltages.shape[2]
    samples = voltages.shape[3]
    inputs = 128 * per_dev
    coefs = jnp.asarray(prototype())
    table = jnp.asarray(quarter_tables())
    y, z, x, core = [
        lax.axis_index(a).astype(jnp.int32).reshape(1) for a in (("yh", "yl"), "z", "x", "c")
    ]
    stream = voltages.reshape(BLKS * per_dev, samples)
    quarter = samples // 4
    tile = (SUB, LANES)
    tables = [whole(TAPS, NFFT), pl.BlockSpec(memory_space=pl.ANY)]
    table_scratch = [pltpu.VMEM((4, DEVICES, HALF), BF16), pltpu.SemaphoreType.DMA]

    slab = (FLAT // 2,) + tile
    owners = (4, RING, SUB) + tile
    last_shapes = [(3, 2) + slab, (4, 2) + slab, slab, slab, owners]
    own, other, far, near, tail = call(
        last_frames, (BLKS // 2,),
        [
            SMEM, SMEM, SMEM, SMEM,
            pl.BlockSpec((16, quarter), lambda g: (g, 3)),
            pl.BlockSpec((16, quarter), lambda g: (g, 2)),
        ] + tables,
        [IN_VMEM] * 5, [pltpu.VMEM(s, BF16) for s in last_shapes],
        [
            pltpu.VMEM((2, HALF // LANES, 256, LANES), F32),
            pltpu.VMEM((2, HALF // LANES, (TAPS - 1) * 80, LANES), F32),
            pltpu.VMEM((4, 512, HALF), BF16),
            pltpu.VMEM((4, DEVICES, 512), F32),
            pltpu.VMEM((16, FLAT * SUB, LANES), F32),
        ] + table_scratch,
        "last_frames", 56,
    )(y, z, core, input_gains, stream, stream, coefs, table)
    tail = along(tail, "yh", 1, 2)
    other = along(other, "c", 1, 2)
    main_gains, other = lax.optimization_barrier((input_gains, other))
    far = along_ring(jnp.stack([far, other[3, 0]]), 4)
    ring = [along_ring(jnp.stack([own[j], other[j]], axis=1), j + 1) for j in range(3)]

    main = call(
        main_frames, (BLKS // 2,),
        [
            SMEM,
            pl.BlockSpec((16, 2 * quarter), lambda g: (g, 0)),
            pl.BlockSpec((16, quarter), lambda g: (g, 2)),
        ] + tables,
        IN_VMEM, pltpu.VMEM((3,) + owners, BF16),
        [
            pltpu.VMEM((2, HALF // LANES, 768, LANES), F32),
            pltpu.VMEM((4, 768, HALF), BF16),
            pltpu.VMEM((4, DEVICES, 768), F32),
            pltpu.VMEM((3 * RING, FLAT * SUB, LANES), F32),
        ] + table_scratch,
        "main_frames", 52,
    )(main_gains, stream, stream, coefs, table)
    ring, far, tail, main = lax.optimization_barrier((ring, far, tail, main))
    packed = (DEVICES, 3) + tile
    main = pl.pallas_call(
        complete, in_specs=[IN_VMEM] * 2, out_specs=IN_VMEM, out_shape=pltpu.VMEM(packed, BF16), name="complete",
        compiler_params=pltpu.CompilerParams(vmem_limit_bytes=8 * MIB),
    )(in_vmem(main.reshape((3, DEVICES) + tile)), in_vmem(tail.reshape((DEVICES,) + tile)))
    main = lax.all_to_all(main, AXES, split_axis=0, concat_axis=0, tiled=True)

    leaving = jnp.stack([lax.dynamic_index_in_dim(a, 1 - core[0], 0, keepdims=False) for a in ring])
    part = along(leaving, "c", 1, 2)
    by_y = simple(
        sort_y, (y, core), (*ring, part, far, near, other[3, 1]), [(16, 4) + tile] * 4, "sort_y"
    )
    by_y = [by_y[0]] + [along(by_y[d], ("yh", "yl"), d, 4) for d in range(1, 4)]
    by_x = simple(sort_x, (x,), by_y, [(4, 16) + tile] * 4, "sort_x")
    by_x = [by_x[0]] + [along(by_x[d], "x", d, 4) for d in range(1, 4)]
    last, = simple(arrange, (y, z, x, core), by_x, [(DEVICES,) + tile], "arrange")

    scale = 1.0 / (BLKS * SPEC * lax.axis_size("yh"))
    block = 512
    return call(
        functools.partial(correlate, scale), (2, inputs // block),
        [whole(*packed), whole(DEVICES, *tile)],
        pl.BlockSpec((1, 2, block, inputs), lambda m, r: (m, 0, r, 0)),
        jax.ShapeDtypeStruct((2, 2, inputs, inputs), BF16),
        [pltpu.VMEM((inputs, 4 * LANES), BF16), pltpu.VMEM((inputs, 4 * LANES), BF16)],
        "correlate", 28,
    )(main, last)


def solution(mesh):
    fine = Mesh(mesh.devices.reshape(2, 2, RING, 4, 2), AXES)
    inputs = ("yl", "z", "x", "c")
    return jax.shard_map(
        on_device, mesh=fine, in_specs=(P(None, "yh", inputs, None), P(inputs)),
        out_specs=P(AXES, None, None, None), check_vma=False,
    )
```

```python
import functools
import math

import jax
import jax.numpy as jnp
import numpy as np
from jax import lax
from jax.experimental import pallas as pl
from jax.experimental.pallas import tpu as pltpu
from jax.sharding import Mesh, PartitionSpec as P

CHANNELS = 512
NFFT = 2048
HALF = NFFT // 2
TAPS = 4
SPEC = 16
BLKS = 8
LANES = 128
SUB = 8
RING = 8
AXES = ("yh", "yl", "z", "x", "c")
DEVICES = 256
FLAT = 32
MIB = 1024 * 1024
BF16 = jnp.bfloat16
F32 = jnp.float32


def prototype():
    positions = np.arange(TAPS * NFFT, dtype=np.float64) + 0.5
    window = 0.5 - 0.5 * np.cos(2.0 * math.pi * positions / (TAPS * NFFT))
    shape_fn = np.sinc(positions / NFFT - TAPS / 2.0) * window
    shape_fn = shape_fn / np.sqrt(TAPS * np.mean(shape_fn * shape_fn))
    return shape_fn.reshape(TAPS, NFFT).astype(np.float32)


def quarter_tables():
    owner = np.arange(DEVICES, dtype=np.int64).reshape(4, RING, 8).swapaxes(0, 1).reshape(DEVICES)
    sample = np.arange(HALF, dtype=np.int64)
    norm = 1.0 / math.sqrt(NFFT)
    quarters = []
    for r in range(2):
        angle = ((2 * owner[:, None] + r) * sample % NFFT) * (2.0 * math.pi / NFFT)
        quarters += [np.cos(angle) * norm, -np.sin(angle) * norm]
    return np.stack(quarters).astype(BF16)


def row_gain(gain_ref):
    row = lax.broadcasted_iota(jnp.int32, (2 * SUB, LANES), 0) % SUB
    gain = jnp.zeros((2 * SUB, LANES), F32)
    for i in range(SUB):
        gain = jnp.where(row == i, gain_ref[i], gain)
    return gain


def filter_frames(load, gain_ref, coef_ref, outputs, emit):
    gain = row_gain(gain_ref)

    def columns(j, carry):
        low = pl.multiple_of(j * LANES, LANES)
        weights = [
            [coef_ref[k : k + 1, pl.ds(low + h * HALF, LANES)] * gain for k in range(TAPS)]
            for h in range(2)
        ]
        held = {}
        for s in outputs:
            sums = []
            for h in range(2):
                total = None
                for k in range(TAPS):
                    frame = s - (TAPS - 1) + k
                    if frame < 0 or frame >= SPEC:
                        continue
                    if (frame, h) not in held:
                        held[frame, h] = load(frame, low + h * HALF).astype(F32)
                    term = held[frame, h] * weights[h][k]
                    total = term if total is None else total + term
                sums.append(total)
            emit(s, j, sums[0] + sums[1], sums[0] - sums[1])
        return carry

    lax.fori_loop(0, HALF // LANES, columns, 0)


def place_rows(rows, half, group, i, j, picked):
    packed = picked.astype(BF16)
    for q in (2 * half, 2 * half + 1):
        at = group * 256 + (i // 4) * LANES + ((i + q) % 4) * 32
        rows[q, at : at + 32, j * LANES : (j + 1) * LANES] = packed


def transform(table, half, rows, spec):
    for q in (2 * half, 2 * half + 1):
        spec[q] = lax.dot_general(
            table[q], rows[q], (((1,), (1,)), ((), ())), preferred_element_type=F32
        )


def owner_tiles(spec, tiles, group, turn, start, count):
    lane = lax.broadcasted_iota(jnp.int32, (1, LANES), 1)
    for i in range(SUB):
        p = i % 4
        at = group * 256 + (i // 4) * LANES
        merged = None
        for r in range(4):
            piece = spec[(r - p) % 4, pl.ds(start, count), at : at + LANES]
            merged = piece if merged is None else jnp.where(lane < 32 * r, merged, piece)
        if (turn - p) % 4:
            merged = pltpu.roll(merged, 32 * ((turn - p) % 4), 1)
        tiles[pl.ds(i, count, stride=SUB), :] = merged


def last_frames(y_ref, z_ref, c_ref, gain_ref, high_ref, mid_ref, coef_ref, table_ref,
                own_ref, other_ref, far_ref, near_ref, tail_ref, frames, extra, rows, spec, tiles, held, sem):
    step = pl.program_id(0)
    slot_row = pl.multiple_of(16 * step + SUB * (y_ref[0] >> 1), SUB)
    fetch = pltpu.make_async_copy(table_ref, held, sem)

    @pl.when(step == 0)
    def _():
        fetch.start()
        extra[...] = jnp.zeros_like(extra)

    def load(frame, low):
        if frame >= 12:
            return high_ref[:, pl.ds(low + (frame - 12) * NFFT, LANES)]
        return mid_ref[:, pl.ds(low + (frame - 8) * NFFT, LANES)]

    def emit(s, j, total, diff):
        if s < SPEC:
            at = pl.ds(pl.multiple_of((s - 12) * 64 + 16 * step, 16), 16)
            frames[0, j, at, :] = total
            frames[1, j, at, :] = diff
        else:
            at = pl.ds(pl.multiple_of((s - SPEC) * 80 + slot_row, SUB), 16)
            extra[0, j, at, :] = total
            extra[1, j, at, :] = diff

    filter_frames(load, gain_ref, coef_ref, range(12, SPEC + TAPS - 1), emit)

    @pl.when(step == pl.num_programs(0) - 1)
    def _():
        for half in range(2):
            for i in range(SUB):
                for j in range(HALF // LANES):
                    place_rows(rows, half, 0, i, j, frames[half, j, pl.ds(i, 32, stride=SUB), :])
                    picked = jnp.concatenate(
                        [extra[half, j, pl.ds(80 * s + i, 8, stride=SUB), :] for s in range(TAPS - 1)]
                        + [jnp.zeros((8, LANES), F32)],
                        axis=0,
                    )
                    place_rows(rows, half, 1, i, j, picked)
            if half == 0:
                fetch.wait()
            transform(held, half, rows, spec)
        core = c_ref[0]
        sign = 1 - 2 * core
        for slot, away in enumerate((1, 2, 3, -1, -2, -3, 4, 0)):
            zdest = (z_ref[0] + (sign * away if slot < 6 else away) + RING) & (RING - 1)
            tile = tiles.at[slot]
            owner_tiles(spec, tile, 0, 3, pl.multiple_of(zdest * FLAT, FLAT), FLAT)
            parts = tile[...].reshape(FLAT // 2, 2, SUB, LANES).astype(BF16)
            if slot < 3:
                for owner_core in range(2):
                    own_ref[slot, owner_core] = parts[:, owner_core]
            elif slot < 6:
                for owner_core in range(2):
                    other_ref[slot - 3, owner_core] = parts[:, owner_core]
            else:
                kept_ref = far_ref if slot == 6 else near_ref
                for owner_core in range(2):
                    @pl.when(core == owner_core)
                    def _(owner_core=owner_core):
                        kept_ref[...] = parts[:, owner_core]
                        other_ref[3, slot - 6] = parts[:, 1 - owner_core]
        store_owners(spec, tiles, 8, 1, 0, tail_ref)


def store_owners(spec, tiles, first, group, turn, out_ref):
    for z in range(RING):
        tile = tiles.at[first + z]
        owner_tiles(spec, tile, group, turn, z * FLAT, FLAT)
        out_ref[:, z] = tile[...].reshape(4, SUB, SUB, LANES).astype(BF16)


def main_frames(gain_ref, v_ref, coef_ref, table_ref, out_ref, frames, rows, spec, tiles, held, sem):
    step = pl.program_id(0)
    fetch = pltpu.make_async_copy(table_ref, held, sem)
    pl.when(step == 0)(fetch.start)

    def load(frame, low):
        return v_ref[:, pl.ds(low + frame * NFFT, LANES)]

    def emit(s, j, total, diff):
        at = pl.ds(pl.multiple_of(s * 64 + 16 * step, 16), 16)
        frames[0, j, at, :] = total
        frames[1, j, at, :] = diff

    filter_frames(load, gain_ref, coef_ref, range(12), emit)

    @pl.when(step == pl.num_programs(0) - 1)
    def _():
        for half in range(2):
            for group in range(3):
                for i in range(SUB):
                    for j in range(HALF // LANES):
                        picked = frames[half, j, pl.ds(group * 256 + i, 32, stride=SUB), :]
                        place_rows(rows, half, group, i, j, picked)
            if half == 0:
                fetch.wait()
            transform(held, half, rows, spec)
        for group in range(3):
            store_owners(spec, tiles, RING * group, group, group, out_ref.at[group])


def complete(main_ref, tail_ref, out_ref):
    first = main_ref[0].astype(F32) + tail_ref[...].astype(F32)
    out_ref[:, 0] = first.astype(BF16)
    for group in range(1, 3):
        out_ref[:, group] = main_ref[group]


def sort_y(y_ref, c_ref, one_ref, two_ref, three_ref, part_ref, far_ref, near_ref, next_ref,
           out0_ref, out1_ref, out2_ref, out3_ref):
    core = c_ref[0]
    for dy, out_ref in enumerate((out0_ref, out1_ref, out2_ref, out3_ref)):
        at = pl.ds(((y_ref[0] + dy) & 3) * 4, 4)
        for j, ref in enumerate((one_ref, two_ref, three_ref)):
            for r in range(2):
                out_ref[2 * j + r] = ref[core, r, at]
                out_ref[6 + 2 * j + r] = part_ref[j, r, at]
        for r in range(2):
            out_ref[12 + r] = far_ref[r, at]
        out_ref[14] = near_ref[at]
        out_ref[15] = next_ref[at]


def sort_x(x_ref, a0_ref, a1_ref, a2_ref, a3_ref, out0_ref, out1_ref, out2_ref, out3_ref):
    for dx, out_ref in enumerate((out0_ref, out1_ref, out2_ref, out3_ref)):
        owner_x = (x_ref[0] + dx) & 3
        for dy, ref in enumerate((a0_ref, a1_ref, a2_ref, a3_ref)):
            out_ref[dy] = ref[:, owner_x]


def arrange(y_ref, z_ref, x_ref, c_ref, a0_ref, a1_ref, a2_ref, a3_ref, out_ref):
    y, z, x, core = y_ref[0], z_ref[0], x_ref[0], c_ref[0]
    sign = 1 - 2 * core
    origin = []
    for j in range(3):
        origin += [(-sign * (j + 1), core), (-sign * (j + 1), 1 - core)]
    for j in range(3):
        origin += [(sign * (j + 1), 1 - core), (sign * (j + 1), core)]
    origin += [(4, core), (4, 1 - core), (0, core), (0, 1 - core)]
    for dx, ref in enumerate((a0_ref, a1_ref, a2_ref, a3_ref)):
        xsrc = (x - dx + 4) & 3
        for dy in range(4):
            ysrc = (y - dy + 4) & 3
            for k, (away, source_core) in enumerate(origin):
                zsrc = (z + away + RING) & (RING - 1)
                out_ref[((ysrc * RING + zsrc) * 4 + xsrc) * 2 + source_core] = ref[dy, k]


def correlate(scale, main_ref, last_ref, out_ref, left, swap, corner):
    item = pl.program_id(0)
    block = pl.program_id(1)
    half = DEVICES // 2

    def collect(which):
        lane = lax.broadcasted_iota(jnp.int32, (1, LANES), 1)
        rows = left.shape[0]
        for t in range(2):
            here = slice(t * half, (t + 1) * half)
            groups = [main_ref[here, g] for g in range(3)] + [last_ref[here]]
            groups = [g.astype(F32).reshape(rows, LANES) for g in groups]

            def quarter(q):
                merged = None
                for r in range(4):
                    piece = groups[(r - q) % 4]
                    merged = piece if merged is None else jnp.where(lane < 32 * r, merged, piece)
                return merged

            real = quarter(2 * which)
            imag = pltpu.roll(quarter(2 * which + 1), LANES - 32, 1)
            first = slice(2 * t * LANES, (2 * t + 1) * LANES)
            second = slice((2 * t + 1) * LANES, (2 * t + 2) * LANES)
            left[:, first] = real.astype(BF16)
            swap[:, second] = (-real).astype(BF16)
            imag = imag.astype(BF16)
            left[:, second] = imag
            swap[:, first] = imag

    for which in range(2):
        pl.when((block == 0) & (item == which))(functools.partial(collect, which))

    count = out_ref.shape[2]

    @pl.when(block == 0)
    def _():
        for kind, source in enumerate((left, swap)):
            product = scale * lax.dot_general(
                source[:count, :], left[...], (((1,), (1,)), ((), ())), preferred_element_type=F32
            )
            out_ref[0, kind] = product.astype(BF16)
            corner[kind] = product[:, count:]

    @pl.when(block == 1)
    def _():
        for kind, source in enumerate((left, swap)):
            product = scale * lax.dot_general(
                source[count:, :], left[count:, :], (((1,), (1,)), ((), ())), preferred_element_type=F32
            )
            out_ref[0, kind, :, count:] = product.astype(BF16)
            turned = corner[kind].T
            out_ref[0, kind, :, :count] = (-turned if kind else turned).astype(BF16)


def along_ring(block, distance):
    route = []
    for z in range(RING):
        for c in range(2):
            target = (z + (distance if c == 0 else -distance)) % RING
            route.append((z * 2 + c, target * 2 + c))
    return lax.ppermute(block, ("z", "c"), route)


def along(block, axis, distance, size):
    return lax.ppermute(block, axis, [(i, (i + distance) % size) for i in range(size)])


def call(kernel, grid, in_specs, out_specs, out_shape, scratch, name, limit):
    return pl.pallas_call(
        kernel, grid=grid, in_specs=in_specs, out_specs=out_specs, out_shape=out_shape,
        scratch_shapes=scratch, name=name,
        compiler_params=pltpu.CompilerParams(vmem_limit_bytes=limit * MIB),
    )


def whole(*shape):
    return pl.BlockSpec(shape, lambda *ids: (0,) * len(shape))


SMEM = pl.BlockSpec(memory_space=pltpu.SMEM)
IN_VMEM = pl.BlockSpec(memory_space=pltpu.VMEM)


def in_vmem(array):
    return pltpu.with_memory_space_constraint(array, pltpu.VMEM)


def simple(kernel, scalars, arrays, shapes, name):
    return call(
        kernel, (1,), [SMEM] * len(scalars) + [whole(*a.shape) for a in arrays],
        [whole(*s) for s in shapes], [jax.ShapeDtypeStruct(s, BF16) for s in shapes], [], name, 8,
    )(*scalars, *arrays)


def on_device(voltages, input_gains):
    per_dev = voltages.shape[2]
    samples = voltages.shape[3]
    inputs = 128 * per_dev
    coefs = jnp.asarray(prototype())
    table = jnp.asarray(quarter_tables())
    y, z, x, core = [
        lax.axis_index(a).astype(jnp.int32).reshape(1) for a in (("yh", "yl"), "z", "x", "c")
    ]
    stream = voltages.reshape(BLKS * per_dev, samples)
    quarter = samples // 4
    tile = (SUB, LANES)
    tables = [whole(TAPS, NFFT), pl.BlockSpec(memory_space=pl.ANY)]
    table_scratch = [pltpu.VMEM((4, DEVICES, HALF), BF16), pltpu.SemaphoreType.DMA]

    slab = (FLAT // 2,) + tile
    owners = (4, RING, SUB) + tile
    last_shapes = [(3, 2) + slab, (4, 2) + slab, slab, slab, owners]
    own, other, far, near, tail = call(
        last_frames, (BLKS // 2,),
        [
            SMEM, SMEM, SMEM, SMEM,
            pl.BlockSpec((16, quarter), lambda g: (g, 3)),
            pl.BlockSpec((16, quarter), lambda g: (g, 2)),
        ] + tables,
        [IN_VMEM] * 5, [pltpu.VMEM(s, BF16) for s in last_shapes],
        [
            pltpu.VMEM((2, HALF // LANES, 256, LANES), F32),
            pltpu.VMEM((2, HALF // LANES, (TAPS - 1) * 80, LANES), F32),
            pltpu.VMEM((4, 512, HALF), BF16),
            pltpu.VMEM((4, DEVICES, 512), F32),
            pltpu.VMEM((16, FLAT * SUB, LANES), F32),
        ] + table_scratch,
        "last_frames", 56,
    )(y, z, core, input_gains, stream, stream, coefs, table)
    tail = along(tail, "yh", 1, 2)
    other = along(other, "c", 1, 2)
    main_gains, other = lax.optimization_barrier((input_gains, other))
    far = along_ring(jnp.stack([far, other[3, 0]]), 4)
    ring = [along_ring(jnp.stack([own[j], other[j]], axis=1), j + 1) for j in range(3)]

    main = call(
        main_frames, (BLKS // 2,),
        [
            SMEM, pl.BlockSpec((16, samples), lambda g: (g, 0)),
        ] + tables,
        IN_VMEM, pltpu.VMEM((3,) + owners, BF16),
        [
            pltpu.VMEM((2, HALF // LANES, 768, LANES), F32),
            pltpu.VMEM((4, 768, HALF), BF16),
            pltpu.VMEM((4, DEVICES, 768), F32),
            pltpu.VMEM((3 * RING, FLAT * SUB, LANES), F32),
        ] + table_scratch,
        "main_frames", 38,
    )(main_gains, stream, coefs, table)
    packed = (DEVICES, 3) + tile
    main = pl.pallas_call(
        complete, in_specs=[IN_VMEM] * 2, out_specs=IN_VMEM, out_shape=pltpu.VMEM(packed, BF16), name="complete",
        compiler_params=pltpu.CompilerParams(vmem_limit_bytes=8 * MIB),
    )(in_vmem(main.reshape((3, DEVICES) + tile)), in_vmem(tail.reshape((DEVICES,) + tile)))
    far, ring, main = lax.optimization_barrier((far, ring, main))
    main = lax.all_to_all(main, AXES, split_axis=0, concat_axis=0, tiled=True)

    leaving = jnp.stack([lax.dynamic_index_in_dim(a, 1 - core[0], 0, keepdims=False) for a in ring])
    part = along(leaving, "c", 1, 2)
    by_y = simple(
        sort_y, (y, core), (*ring, part, far, near, other[3, 1]), [(16, 4) + tile] * 4, "sort_y"
    )
    by_y = [by_y[0]] + [along(by_y[d], ("yh", "yl"), d, 4) for d in range(1, 4)]
    by_x = simple(sort_x, (x,), by_y, [(4, 16) + tile] * 4, "sort_x")
    by_x = [by_x[0]] + [along(by_x[d], "x", d, 4) for d in range(1, 4)]
    last, = simple(arrange, (y, z, x, core), by_x, [(DEVICES,) + tile], "arrange")

    scale = 1.0 / (BLKS * SPEC * lax.axis_size("yh"))
    block = inputs // 2
    return call(
        functools.partial(correlate, scale), (2, 2),
        [whole(*packed), whole(DEVICES, *tile)],
        pl.BlockSpec((1, 2, block, inputs), lambda m, r: (m, 0, r, 0)),
        jax.ShapeDtypeStruct((2, 2, inputs, inputs), BF16),
        [pltpu.VMEM((inputs, 4 * LANES), BF16)] * 2 + [pltpu.VMEM((2, block, block), F32)],
        "correlate", 28,
    )(main, last)


def solution(mesh):
    fine = Mesh(mesh.devices.reshape(2, 2, RING, 4, 2), AXES)
    inputs = ("yl", "z", "x", "c")
    return jax.shard_map(
        on_device, mesh=fine, in_specs=(P(None, "yh", inputs, None), P(inputs)),
        out_specs=P(AXES, None, None, None), check_vma=False,
    )
```

```python
import functools
import math

import jax
import jax.numpy as jnp
import numpy as np
from jax import lax
from jax.experimental import pallas as pl
from jax.experimental.pallas import tpu as pltpu
from jax.sharding import Mesh, PartitionSpec as P

CHANNELS = 512
NFFT = 2048
HALF = NFFT // 2
TAPS = 4
SPEC = 16
BLKS = 8
LANES = 128
SUB = 8
RING = 8
AXES = ("yh", "yl", "z", "x", "c")
DEVICES = 256
FLAT = 32
MIB = 1024 * 1024
BF16 = jnp.bfloat16
F32 = jnp.float32


def prototype():
    positions = np.arange(TAPS * NFFT, dtype=np.float64) + 0.5
    window = 0.5 - 0.5 * np.cos(2.0 * math.pi * positions / (TAPS * NFFT))
    shape_fn = np.sinc(positions / NFFT - TAPS / 2.0) * window
    shape_fn = shape_fn / np.sqrt(TAPS * np.mean(shape_fn * shape_fn))
    return shape_fn.reshape(TAPS, NFFT).astype(np.float32)


def quarter_tables():
    owner = np.arange(DEVICES, dtype=np.int64).reshape(4, RING, 8).swapaxes(0, 1).reshape(DEVICES)
    sample = np.arange(HALF, dtype=np.int64)
    norm = 1.0 / math.sqrt(NFFT)
    quarters = []
    for r in range(2):
        angle = ((2 * owner[:, None] + r) * sample % NFFT) * (2.0 * math.pi / NFFT)
        quarters += [np.cos(angle) * norm, -np.sin(angle) * norm]
    return np.stack(quarters).astype(BF16)


def row_gain(gain_ref):
    row = lax.broadcasted_iota(jnp.int32, (2 * SUB, LANES), 0) % SUB
    gain = jnp.zeros((2 * SUB, LANES), F32)
    for i in range(SUB):
        gain = jnp.where(row == i, gain_ref[i], gain)
    return gain


def filter_frames(load, gain_ref, coef_ref, outputs, emit):
    gain = row_gain(gain_ref)

    def columns(j, carry):
        low = pl.multiple_of(j * LANES, LANES)
        weights = [
            [coef_ref[k : k + 1, pl.ds(low + h * HALF, LANES)] * gain for k in range(TAPS)]
            for h in range(2)
        ]
        held = {}
        for s in outputs:
            sums = []
            for h in range(2):
                total = None
                for k in range(TAPS):
                    frame = s - (TAPS - 1) + k
                    if frame < 0 or frame >= SPEC:
                        continue
                    if (frame, h) not in held:
                        held[frame, h] = load(frame, low + h * HALF).astype(F32)
                    term = held[frame, h] * weights[h][k]
                    total = term if total is None else total + term
                sums.append(total)
            emit(s, j, sums[0] + sums[1], sums[0] - sums[1])
        return carry

    lax.fori_loop(0, HALF // LANES, columns, 0)


def place_rows(rows, half, group, i, j, picked):
    packed = picked.astype(BF16)
    for q in (2 * half, 2 * half + 1):
        at = group * 256 + (i // 4) * LANES + ((i + q) % 4) * 32
        rows[q, at : at + 32, j * LANES : (j + 1) * LANES] = packed


def transform(table, half, rows, spec):
    for q in (2 * half, 2 * half + 1):
        spec[q] = lax.dot_general(
            table[q], rows[q], (((1,), (1,)), ((), ())), preferred_element_type=F32
        )


def owner_tiles(spec, tiles, group, turn, start, count):
    lane = lax.broadcasted_iota(jnp.int32, (1, LANES), 1)
    for i in range(SUB):
        p = i % 4
        at = group * 256 + (i // 4) * LANES
        merged = None
        for r in range(4):
            piece = spec[(r - p) % 4, pl.ds(start, count), at : at + LANES]
            merged = piece if merged is None else jnp.where(lane < 32 * r, merged, piece)
        if (turn - p) % 4:
            merged = pltpu.roll(merged, 32 * ((turn - p) % 4), 1)
        tiles[pl.ds(i, count, stride=SUB), :] = merged


def last_frames(y_ref, z_ref, c_ref, gain_ref, high_ref, mid_ref, coef_ref, table_ref,
                own_ref, other_ref, far_ref, near_ref, tail_ref, held, frames, extra, rows, spec, tiles, sem):
    step = pl.program_id(0)
    slot_row = pl.multiple_of(16 * step + SUB * (y_ref[0] >> 1), SUB)
    fetch = pltpu.make_async_copy(table_ref, held, sem)

    @pl.when(step == 0)
    def _():
        fetch.start()
        extra[...] = jnp.zeros_like(extra)

    def load(frame, low):
        if frame >= 12:
            return high_ref[:, pl.ds(low + (frame - 12) * NFFT, LANES)]
        return mid_ref[:, pl.ds(low + (frame - 8) * NFFT, LANES)]

    def emit(s, j, total, diff):
        if s < SPEC:
            at = pl.ds(pl.multiple_of((s - 12) * 64 + 16 * step, 16), 16)
            frames[0, j, at, :] = total
            frames[1, j, at, :] = diff
        else:
            at = pl.ds(pl.multiple_of((s - SPEC) * 80 + slot_row, SUB), 16)
            extra[0, j, at, :] = total
            extra[1, j, at, :] = diff

    filter_frames(load, gain_ref, coef_ref, range(12, SPEC + TAPS - 1), emit)

    @pl.when(step == pl.num_programs(0) - 1)
    def _():
        for half in range(2):
            for i in range(SUB):
                for j in range(HALF // LANES):
                    place_rows(rows, half, 0, i, j, frames[half, j, pl.ds(i, 32, stride=SUB), :])
                    picked = jnp.concatenate(
                        [extra[half, j, pl.ds(80 * s + i, 8, stride=SUB), :] for s in range(TAPS - 1)]
                        + [jnp.zeros((8, LANES), F32)],
                        axis=0,
                    )
                    place_rows(rows, half, 1, i, j, picked)
            if half == 0:
                fetch.wait()
            transform(held, half, rows, spec)
        core = c_ref[0]
        sign = 1 - 2 * core
        for slot, away in enumerate((1, 2, 3, -1, -2, -3, 4, 0)):
            zdest = (z_ref[0] + (sign * away if slot < 6 else away) + RING) & (RING - 1)
            tile = tiles.at[slot]
            owner_tiles(spec, tile, 0, 3, pl.multiple_of(zdest * FLAT, FLAT), FLAT)
            parts = tile[...].reshape(FLAT // 2, 2, SUB, LANES).astype(BF16)
            if slot < 3:
                for owner_core in range(2):
                    own_ref[slot, owner_core] = parts[:, owner_core]
            elif slot < 6:
                for owner_core in range(2):
                    other_ref[slot - 3, owner_core] = parts[:, owner_core]
            else:
                kept_ref = far_ref if slot == 6 else near_ref
                for owner_core in range(2):
                    @pl.when(core == owner_core)
                    def _(owner_core=owner_core):
                        kept_ref[...] = parts[:, owner_core]
                        other_ref[3, slot - 6] = parts[:, 1 - owner_core]
        store_owners(spec, tiles, 8, 1, 0, tail_ref)


def store_owners(spec, tiles, first, group, turn, out_ref):
    for z in range(RING):
        tile = tiles.at[first + z]
        owner_tiles(spec, tile, group, turn, z * FLAT, FLAT)
        out_ref[:, z] = tile[...].reshape(4, SUB, SUB, LANES).astype(BF16)


def main_frames(gain_ref, v_ref, coef_ref, held, out_ref, frames, rows, spec, tiles):
    step = pl.program_id(0)

    def load(frame, low):
        return v_ref[:, pl.ds(low + frame * NFFT, LANES)]

    def emit(s, j, total, diff):
        at = pl.ds(pl.multiple_of(s * 64 + 16 * step, 16), 16)
        frames[0, j, at, :] = total
        frames[1, j, at, :] = diff

    filter_frames(load, gain_ref, coef_ref, range(12), emit)

    @pl.when(step == pl.num_programs(0) - 1)
    def _():
        for half in range(2):
            for group in range(3):
                for i in range(SUB):
                    for j in range(HALF // LANES):
                        picked = frames[half, j, pl.ds(group * 256 + i, 32, stride=SUB), :]
                        place_rows(rows, half, group, i, j, picked)
            transform(held, half, rows, spec)
        for group in range(3):
            store_owners(spec, tiles, RING * group, group, group, out_ref.at[group])


def complete(main_ref, tail_ref, out_ref):
    first = main_ref[0].astype(F32) + tail_ref[...].astype(F32)
    out_ref[:, 0] = first.astype(BF16)
    for group in range(1, 3):
        out_ref[:, group] = main_ref[group]


def sort_y(y_ref, c_ref, one_ref, two_ref, three_ref, part_ref, far_ref, near_ref, next_ref,
           out0_ref, out1_ref, out2_ref, out3_ref):
    core = c_ref[0]
    for dy, out_ref in enumerate((out0_ref, out1_ref, out2_ref, out3_ref)):
        at = pl.ds(((y_ref[0] + dy) & 3) * 4, 4)
        for j, ref in enumerate((one_ref, two_ref, three_ref)):
            for r in range(2):
                out_ref[2 * j + r] = ref[core, r, at]
                out_ref[6 + 2 * j + r] = part_ref[j, r, at]
        for r in range(2):
            out_ref[12 + r] = far_ref[r, at]
        out_ref[14] = near_ref[at]
        out_ref[15] = next_ref[at]


def sort_x(x_ref, a0_ref, a1_ref, a2_ref, a3_ref, out0_ref, out1_ref, out2_ref, out3_ref):
    for dx, out_ref in enumerate((out0_ref, out1_ref, out2_ref, out3_ref)):
        owner_x = (x_ref[0] + dx) & 3
        for dy, ref in enumerate((a0_ref, a1_ref, a2_ref, a3_ref)):
            out_ref[dy] = ref[:, owner_x]


def arrange(y_ref, z_ref, x_ref, c_ref, a0_ref, a1_ref, a2_ref, a3_ref, out_ref):
    y, z, x, core = y_ref[0], z_ref[0], x_ref[0], c_ref[0]
    sign = 1 - 2 * core
    origin = []
    for j in range(3):
        origin += [(-sign * (j + 1), core), (-sign * (j + 1), 1 - core)]
    for j in range(3):
        origin += [(sign * (j + 1), 1 - core), (sign * (j + 1), core)]
    origin += [(4, core), (4, 1 - core), (0, core), (0, 1 - core)]
    for dx, ref in enumerate((a0_ref, a1_ref, a2_ref, a3_ref)):
        xsrc = (x - dx + 4) & 3
        for dy in range(4):
            ysrc = (y - dy + 4) & 3
            for k, (away, source_core) in enumerate(origin):
                zsrc = (z + away + RING) & (RING - 1)
                out_ref[((ysrc * RING + zsrc) * 4 + xsrc) * 2 + source_core] = ref[dy, k]


def correlate(scale, main_ref, last_ref, out_ref, left, swap, corner):
    item = pl.program_id(0)
    block = pl.program_id(1)
    half = DEVICES // 2

    def collect(which):
        lane = lax.broadcasted_iota(jnp.int32, (1, LANES), 1)
        rows = left.shape[0]
        for t in range(2):
            here = slice(t * half, (t + 1) * half)
            groups = [main_ref[here, g] for g in range(3)] + [last_ref[here]]
            groups = [g.astype(F32).reshape(rows, LANES) for g in groups]

            def quarter(q):
                merged = None
                for r in range(4):
                    piece = groups[(r - q) % 4]
                    merged = piece if merged is None else jnp.where(lane < 32 * r, merged, piece)
                return merged

            real = quarter(2 * which)
            imag = pltpu.roll(quarter(2 * which + 1), LANES - 32, 1)
            first = slice(2 * t * LANES, (2 * t + 1) * LANES)
            second = slice((2 * t + 1) * LANES, (2 * t + 2) * LANES)
            left[:, first] = real.astype(BF16)
            swap[:, second] = (-real).astype(BF16)
            imag = imag.astype(BF16)
            left[:, second] = imag
            swap[:, first] = imag

    for which in range(2):
        pl.when((block == 0) & (item == which))(functools.partial(collect, which))

    count = out_ref.shape[2]

    @pl.when(block == 0)
    def _():
        for kind, source in enumerate((left, swap)):
            product = scale * lax.dot_general(
                source[:count, :], left[...], (((1,), (1,)), ((), ())), preferred_element_type=F32
            )
            out_ref[0, kind] = product.astype(BF16)
            corner[kind] = product[:, count:]

    @pl.when(block == 1)
    def _():
        for kind, source in enumerate((left, swap)):
            product = scale * lax.dot_general(
                source[count:, :], left[count:, :], (((1,), (1,)), ((), ())), preferred_element_type=F32
            )
            out_ref[0, kind, :, count:] = product.astype(BF16)
            turned = corner[kind].T
            out_ref[0, kind, :, :count] = (-turned if kind else turned).astype(BF16)


def along_ring(block, distance):
    route = []
    for z in range(RING):
        for c in range(2):
            target = (z + (distance if c == 0 else -distance)) % RING
            route.append((z * 2 + c, target * 2 + c))
    return lax.ppermute(block, ("z", "c"), route)


def along(block, axis, distance, size):
    return lax.ppermute(block, axis, [(i, (i + distance) % size) for i in range(size)])


def call(kernel, grid, in_specs, out_specs, out_shape, scratch, name, limit):
    return pl.pallas_call(
        kernel, grid=grid, in_specs=in_specs, out_specs=out_specs, out_shape=out_shape,
        scratch_shapes=scratch, name=name,
        compiler_params=pltpu.CompilerParams(vmem_limit_bytes=limit * MIB),
    )


def whole(*shape):
    return pl.BlockSpec(shape, lambda *ids: (0,) * len(shape))


SMEM = pl.BlockSpec(memory_space=pltpu.SMEM)
IN_VMEM = pl.BlockSpec(memory_space=pltpu.VMEM)


def in_vmem(array):
    return pltpu.with_memory_space_constraint(array, pltpu.VMEM)


def simple(kernel, scalars, arrays, shapes, name):
    return call(
        kernel, (1,), [SMEM] * len(scalars) + [whole(*a.shape) for a in arrays],
        [whole(*s) for s in shapes], [jax.ShapeDtypeStruct(s, BF16) for s in shapes], [], name, 8,
    )(*scalars, *arrays)


def on_device(voltages, input_gains):
    per_dev = voltages.shape[2]
    samples = voltages.shape[3]
    inputs = 128 * per_dev
    coefs = jnp.asarray(prototype())
    table = jnp.asarray(quarter_tables())
    y, z, x, core = [
        lax.axis_index(a).astype(jnp.int32).reshape(1) for a in (("yh", "yl"), "z", "x", "c")
    ]
    stream = voltages.reshape(BLKS * per_dev, samples)
    quarter = samples // 4
    tile = (SUB, LANES)
    tables = [whole(TAPS, NFFT), pl.BlockSpec(memory_space=pl.ANY)]

    slab = (FLAT // 2,) + tile
    owners = (4, RING, SUB) + tile
    last_shapes = [(3, 2) + slab, (4, 2) + slab, slab, slab, owners, (4, DEVICES, HALF)]
    own, other, far, near, tail, held_table = call(
        last_frames, (BLKS // 2,),
        [
            SMEM, SMEM, SMEM, SMEM,
            pl.BlockSpec((16, quarter), lambda g: (g, 3)),
            pl.BlockSpec((16, quarter), lambda g: (g, 2)),
        ] + tables,
        [IN_VMEM] * 6, [pltpu.VMEM(s, BF16) for s in last_shapes],
        [
            pltpu.VMEM((2, HALF // LANES, 256, LANES), F32),
            pltpu.VMEM((2, HALF // LANES, (TAPS - 1) * 80, LANES), F32),
            pltpu.VMEM((4, 512, HALF), BF16),
            pltpu.VMEM((4, DEVICES, 512), F32),
            pltpu.VMEM((16, FLAT * SUB, LANES), F32),
            pltpu.SemaphoreType.DMA,
        ],
        "last_frames", 56,
    )(y, z, core, input_gains, stream, stream, coefs, table)
    tail = along(tail, "yh", 1, 2)
    other = along(other, "c", 1, 2)
    main_gains, other = lax.optimization_barrier((input_gains, other))
    far = along_ring(jnp.stack([far, other[3, 0]]), 4)
    ring = [along_ring(jnp.stack([own[j], other[j]], axis=1), j + 1) for j in range(3)]

    main = call(
        main_frames, (BLKS // 2,),
        [
            SMEM, pl.BlockSpec((16, samples), lambda g: (g, 0)), tables[0], IN_VMEM,
        ],
        IN_VMEM, pltpu.VMEM((3,) + owners, BF16),
        [
            pltpu.VMEM((2, HALF // LANES, 768, LANES), F32),
            pltpu.VMEM((4, 768, HALF), BF16),
            pltpu.VMEM((4, DEVICES, 768), F32),
            pltpu.VMEM((3 * RING, FLAT * SUB, LANES), F32),
        ],
        "main_frames", 38,
    )(main_gains, stream, coefs, in_vmem(held_table))
    packed = (DEVICES, 3) + tile
    main = pl.pallas_call(
        complete, in_specs=[IN_VMEM] * 2, out_specs=IN_VMEM, out_shape=pltpu.VMEM(packed, BF16), name="complete",
        compiler_params=pltpu.CompilerParams(vmem_limit_bytes=8 * MIB),
    )(in_vmem(main.reshape((3, DEVICES) + tile)), in_vmem(tail.reshape((DEVICES,) + tile)))
    far, ring, main = lax.optimization_barrier((far, ring, main))
    main = lax.all_to_all(main, AXES, split_axis=0, concat_axis=0, tiled=True)

    leaving = jnp.stack([lax.dynamic_index_in_dim(a, 1 - core[0], 0, keepdims=False) for a in ring])
    part = along(leaving, "c", 1, 2)
    by_y = simple(
        sort_y, (y, core), (*ring, part, far, near, other[3, 1]), [(16, 4) + tile] * 4, "sort_y"
    )
    by_y = [by_y[0]] + [along(by_y[d], ("yh", "yl"), d, 4) for d in range(1, 4)]
    by_x = simple(sort_x, (x,), by_y, [(4, 16) + tile] * 4, "sort_x")
    by_x = [by_x[0]] + [along(by_x[d], "x", d, 4) for d in range(1, 4)]
    last, = simple(arrange, (y, z, x, core), by_x, [(DEVICES,) + tile], "arrange")

    scale = 1.0 / (BLKS * SPEC * lax.axis_size("yh"))
    block = inputs // 2
    return call(
        functools.partial(correlate, scale), (2, 2),
        [whole(*packed), whole(DEVICES, *tile)],
        pl.BlockSpec((1, 2, block, inputs), lambda m, r: (m, 0, r, 0)),
        jax.ShapeDtypeStruct((2, 2, inputs, inputs), BF16),
        [pltpu.VMEM((inputs, 4 * LANES), BF16)] * 2 + [pltpu.VMEM((2, block, block), F32)],
        "correlate", 28,
    )(main, last)


def solution(mesh):
    fine = Mesh(mesh.devices.reshape(2, 2, RING, 4, 2), AXES)
    inputs = ("yl", "z", "x", "c")
    return jax.shard_map(
        on_device, mesh=fine, in_specs=(P(None, "yh", inputs, None), P(inputs)),
        out_specs=P(AXES, None, None, None), check_vma=False,
    )
```
